32 devices in a mesh: groups: 2 (over y), seq: 8 (over z, x), head: 2 (over core).
Axes of the slice: x: 2, y: 2, z: 4, core: 2. Of those that a mesh axis runs over, the one named last changes fastest.
Arguments:
- queries: bfloat16 [2048, 4096], P(('groups', 'seq'), 'head'), parts along dimension 0, may hold values from -6 to 6
- key_rows: bfloat16 [2048, 4096], P(('groups', 'seq'), 'head'), parts along dimension 0, may hold values from -6 to 6
- value_rows: bfloat16 [2048, 4096], P(('groups', 'seq'), 'head'), parts along dimension 0, may hold values from -6 to 6
- out_grad: bfloat16 [2048, 4096], P(('groups', 'seq'), 'head'), parts along dimension 0, may hold values from -6 to 6
- lengths: int32 [32], P('groups'), parts along dimension 0, may hold values from 1 to 256, 1024 in all
Outputs:
- attended: bfloat16 [2048, 4096], P(('groups', 'seq'), 'head'), parts along dimension 0
- query_grad: bfloat16 [2048, 4096], P(('groups', 'seq'), 'head'), parts along dimension 0
- key_grad: bfloat16 [2048, 4096], P(('groups', 'seq'), 'head'), parts along dimension 0
- value_grad: bfloat16 [2048, 4096], P(('groups', 'seq'), 'head'), parts along dimension 0
The draws below stay inside these ranges and needn't reach their ends.
There are 2 independent parts, one for each index of `groups`. The reference program is written for one: setup_inputs(seed, part) draws one part's arguments, and reference() takes and returns one part's arrays. A program takes and returns all parts, laid end to end along the dimension named above; each array names one. Nothing has to cross between parts.
Inputs may be any that keep to these rules, and one draw needn't show every extreme that they name: The lengths sum to 1024; the longest document has exactly 256 tokens.
All inputs are finite; a program needn't handle non-finite values.
Results may differ from the reference program's by a relative error of at most 0.0044.
Values sent between devices are 32-bit elements; how exact they have to be, the bound alone decides.
A program may use at most 64 MiB of HBM per device.

```python
import math
import jax
import jax.numpy as jnp
import numpy as np
from jax import lax

TOK_DEV = 128
HEADS = 32
DH = 128
DOCS = 16
SEQ = 1024
FEAT = 4096


def shard_levels(key, dims, cuts, smallest, high):
    factor_of = 1.0
    for axis_at, shards_of in cuts:
        steps = jax.random.uniform(jax.random.fold_in(jax.random.fold_in(key, 6), axis_at), (shards_of,), jnp.float32, smallest / len(cuts), high / len(cuts))
        factor_of = factor_of * jnp.repeat(jnp.exp(steps), dims[axis_at] // shards_of).reshape((-1,) + (1,) * (len(dims) - 1 - axis_at))
    return factor_of


def split_up(amount, total, limit, slope):
    weights = [(1 << 20) // math.isqrt(grade ** slope) + 1 for grade in range(2, amount + 1)]
    rest, given = total - limit - (amount - 1), [1] * (amount - 1)
    while rest > 0:
        candidates = [i for i in range(amount - 1) if given[i] < limit]
        pool, left = sum([weights[i] for i in candidates]), rest
        for i in candidates:
            extra = min(limit - given[i], max(1, left * weights[i] // pool), rest)
            given[i] = given[i] + extra
            rest = rest - extra
    return np.array([limit] + given)


def uneven(stream_key, number_of, total, limit, slope):
    if number_of == 2:
        one = jax.random.randint(stream_key, (), max(1, total - limit), min(limit, total - 1) + 1)
        return jnp.stack([one, total - one])
    tallies = jnp.asarray(split_up(number_of, total, limit, slope), jnp.int32)
    pairs = (number_of - 1) // 2
    giver, sink = tallies[1:1 + 2 * pairs:2], tallies[2:2 + 2 * pairs:2]
    room = jnp.minimum(giver - 1, limit - sink)
    passed = jax.random.randint(jax.random.fold_in(stream_key, 1), (pairs,), 0, 1 << 20) % (room + 1)
    tallies = tallies.at[1:1 + 2 * pairs:2].set(giver - passed).at[2:2 + 2 * pairs:2].set(sink + passed)
    return tallies[jax.random.permutation(jax.random.fold_in(stream_key, 2), number_of)]


def noise(rng, shape, spread, limit, split=(), held_as=jnp.bfloat16):
    loudness = shard_levels(rng, shape, split, -0.22, 0.18) if split else 1.0
    array = jax.random.normal(rng, shape, jnp.float32) * spread * loudness
    return jnp.minimum(jnp.maximum(array, -limit), limit).astype(held_as)


def setup_inputs(seed: int = 0, part: int = 0) -> dict:
    seeds = jax.random.split(jax.random.key(seed), 6)
    part_splits = jax.random.split(jax.random.fold_in(seeds[5], part), 6)
    return {
        "queries": noise(part_splits[0], (SEQ, FEAT), 1.0, 6.0, ((0, 8), (1, 2))),
        "key_rows": noise(part_splits[1], (SEQ, FEAT), 1.0, 6.0, ((0, 8), (1, 2))),
        "value_rows": noise(part_splits[2], (SEQ, FEAT), 1.0, 6.0, ((0, 8), (1, 2))),
        "out_grad": noise(part_splits[3], (SEQ, FEAT), 1.0, 6.0, ((0, 8), (1, 2))),
        "lengths": uneven(part_splits[4], DOCS, SEQ, SEQ // 4, 2).astype(jnp.int32),
    }


def reference(queries, key_rows, value_rows, out_grad, lengths):
    seq_len = queries.shape[0]
    tokens = TOK_DEV
    count = seq_len // tokens
    highest = lax.Precision.HIGHEST
    doc_total = jnp.sum(lengths).astype(jnp.float32)
    factor = lax.rsqrt(jnp.float32(DH) * doc_total / DOCS)
    doc_ends = jnp.cumsum(lengths).astype(jnp.int32)
    doc_starts = (doc_ends - lengths).astype(jnp.int32)
    positions = jnp.arange(seq_len, dtype=jnp.int32)
    doc_ids = lax.optimization_barrier(jnp.sum((doc_ends[None, :] <= positions[:, None]).astype(jnp.int32), axis=1))
    opens = jnp.any(doc_starts[None, :] == positions[:, None], axis=1)
    doc_blocks = doc_ids.reshape(count, tokens)
    open_blocks = opens.reshape(count, tokens)
    keep_gates = 1.0 - jnp.any(open_blocks, axis=1).astype(jnp.float32)
    open_first = open_blocks[:, 0].astype(jnp.float32)
    open_next = jnp.concatenate([open_first[1:], jnp.zeros((1,), jnp.float32)])
    first_mask = (doc_blocks == doc_blocks[:, :1]).astype(jnp.float32)
    last_mask = (doc_blocks == doc_blocks[:, -1:]).astype(jnp.float32)
    shape4 = (count, tokens, HEADS, DH)
    query_all = queries.reshape(shape4)
    key_all = key_rows.reshape(shape4)
    value_all = value_rows.reshape(shape4)
    grad_all = out_grad.reshape(shape4)
    forward_states = jnp.einsum('cshd,cshe->chde', key_all.astype(jnp.float32) * last_mask[:, :, None, None], value_all.astype(jnp.float32), precision=highest)
    backward_states = jnp.einsum('cthd,cthe->chde', query_all.astype(jnp.float32) * first_mask[:, :, None, None], grad_all.astype(jnp.float32), precision=highest)

    def chain_step(carried, pieces):
        gate_now, state_now = pieces
        return (state_now + gate_now * carried, carried)
    zero_state = jnp.zeros((HEADS, DH, DH), jnp.float32)
    _, prior = lax.scan(chain_step, zero_state, (keep_gates, forward_states))
    _, later_all = lax.scan(chain_step, zero_state, (keep_gates, backward_states), reverse=True)
    prior = prior * (1.0 - open_first)[:, None, None, None]
    later_all = later_all * (1.0 - open_next)[:, None, None, None]
    local_pos = jnp.arange(tokens, dtype=jnp.int32)

    def one_block(pieces):
        query_b, key_b, value_b, grad_b, docs_b, first_b, last_b, prior_b, later_b = pieces
        query_f = query_b.astype(jnp.float32)
        key_f = key_b.astype(jnp.float32)
        value_f = value_b.astype(jnp.float32)
        grad_f = grad_b.astype(jnp.float32)
        local_mask = (local_pos[None, :] <= local_pos[:, None]) & (docs_b[:, None] == docs_b[None, :])
        raw_scores = jnp.einsum('thd,shd->hts', query_f, key_f, precision=highest)
        scores = jnp.where(local_mask[None], factor * raw_scores, 0.0).astype(jnp.bfloat16)
        scores_f = scores.astype(jnp.float32)
        first_f = factor * first_b[:, None, None]
        last_f = factor * last_b[:, None, None]
        attended = jnp.einsum('hts,she->the', scores_f, value_f, precision=highest) + first_f * jnp.einsum('thd,hde->the', query_f, prior_b, precision=highest)
        raw_grad = jnp.einsum('the,she->hts', grad_f, value_f, precision=highest)
        grad_scores = jnp.where(local_mask[None], factor * raw_grad, 0.0).astype(jnp.bfloat16).astype(jnp.float32)
        query_grad = jnp.einsum('hts,shd->thd', grad_scores, key_f, precision=highest) + first_f * jnp.einsum('the,hde->thd', grad_f, prior_b, precision=highest)
        key_grad = jnp.einsum('hts,thd->shd', grad_scores, query_f, precision=highest) + last_f * jnp.einsum('hde,she->shd', later_b, value_f, precision=highest)
        value_grad = jnp.einsum('hts,the->she', scores_f, grad_f, precision=highest) + last_f * jnp.einsum('hde,shd->she', later_b, key_f, precision=highest)
        return (attended.astype(jnp.bfloat16), query_grad.astype(jnp.bfloat16), key_grad.astype(jnp.bfloat16), value_grad.astype(jnp.bfloat16))
    results = lax.map(one_block, (query_all, key_all, value_all, grad_all, doc_blocks, first_mask, last_mask, prior, later_all))
    flat = [piece.reshape(seq_len, HEADS * DH) for piece in results]
    return (flat[0], flat[1], flat[2], flat[3])
```

```python
import functools

import jax
import jax.numpy as jnp
from jax import lax
from jax.experimental import pallas as pl
from jax.experimental.pallas import tpu as pltpu
from jax.sharding import PartitionSpec as P

DH = 128
DOCS = 16


def from_behind(block, axis, distance):
    devices = range(lax.axis_size(axis))
    route = [(i - distance, i) for i in devices if i - distance in devices]
    return lax.ppermute(block, axis, route)


def combine_pair(earlier, latter):
    return (earlier[0] * latter[0], latter[1] + latter[0] * earlier[1])


def prior_bounded(keep_gate, state, levels):
    distances = [1] + [1 << level for level in range(levels)]
    current = (keep_gate, state)
    for counter, distance in enumerate(distances):
        shifted = from_behind((current[0], current[1]), "seq", distance)
        if counter == 0:
            current = shifted
        else:
            current = combine_pair(shifted, current)
    return current[1]


def later_bounded(keep_gate, state, levels):
    distances = [1] + [1 << level for level in range(levels)]
    current = (keep_gate, state)
    for counter, distance in enumerate(distances):
        shifted = from_behind((current[0], current[1]), "seq", -distance)
        if counter == 0:
            current = shifted
        else:
            current = combine_pair(shifted, current)
    return current[1]


def local_general(queries, key_rows, value_rows, out_grad, lengths):
    tokens = queries.shape[0]
    head_count = queries.shape[1] // DH
    shape3 = (tokens, head_count, DH)
    highest = lax.Precision.HIGHEST
    query_heads = queries.reshape(shape3)
    key_heads = key_rows.reshape(shape3)
    value_heads = value_rows.reshape(shape3)
    grad_heads = out_grad.reshape(shape3)
    block_index = lax.axis_index("seq")
    doc_total = jnp.sum(lengths).astype(jnp.float32)
    factor = lax.rsqrt(jnp.float32(DH) * doc_total / DOCS)
    upto = jnp.tri(lengths.shape[0], dtype=jnp.int32)
    doc_ends = jnp.sum(upto * lengths[None, :], axis=1)
    doc_starts = doc_ends - lengths
    first_pos = block_index * tokens
    positions = first_pos + jnp.arange(tokens, dtype=jnp.int32)
    doc_ids = jnp.sum((doc_ends[None, :] <= positions[:, None]).astype(jnp.int32), axis=1)
    opens = jnp.any(doc_starts[None, :] == positions[:, None], axis=1)
    keep_gate = 1.0 - jnp.any(opens).astype(jnp.float32)
    open_here = opens[0].astype(jnp.float32)
    open_next = jnp.any(doc_starts == first_pos + tokens).astype(jnp.float32)
    first_mask = doc_ids == doc_ids[0]
    last_mask = doc_ids == doc_ids[-1]
    local_mask = (positions[None, :] <= positions[:, None]) & (doc_ids[:, None] == doc_ids[None, :])
    zero_half = jnp.zeros((), jnp.bfloat16)
    forward_state = jnp.einsum(
        "shd,she->hde",
        jnp.where(last_mask[:, None, None], key_heads, zero_half),
        value_heads,
        preferred_element_type=jnp.float32,
    )
    backward_state = jnp.einsum(
        "thd,the->hde",
        jnp.where(first_mask[:, None, None], query_heads, zero_half),
        grad_heads,
        preferred_element_type=jnp.float32,
    )
    levels = max(lax.axis_size("seq") // 4 - 1, 0).bit_length()
    prior = prior_bounded(keep_gate, forward_state, levels)
    later_state = later_bounded(keep_gate, backward_state, levels)
    prior = prior * (1.0 - open_here)
    later_state = later_state * (1.0 - open_next)
    first_f = factor * first_mask.astype(jnp.float32)[:, None, None]
    last_f = factor * last_mask.astype(jnp.float32)[:, None, None]
    raw_scores = jnp.einsum(
        "thd,shd->hts", query_heads, key_heads, preferred_element_type=jnp.float32
    )
    scores = jnp.where(local_mask[None], factor * raw_scores, 0.0).astype(jnp.bfloat16)
    attended = jnp.einsum(
        "hts,she->the", scores, value_heads, preferred_element_type=jnp.float32
    ) + first_f * jnp.einsum(
        "thd,hde->the", query_heads.astype(jnp.float32), prior, precision=highest
    )
    raw_grad = jnp.einsum(
        "the,she->hts", grad_heads, value_heads, preferred_element_type=jnp.float32
    )
    grad_scores = jnp.where(local_mask[None], factor * raw_grad, 0.0).astype(jnp.bfloat16)
    query_grad = jnp.einsum(
        "hts,shd->thd", grad_scores, key_heads, preferred_element_type=jnp.float32
    ) + first_f * jnp.einsum(
        "the,hde->thd", grad_heads.astype(jnp.float32), prior, precision=highest
    )
    key_grad = jnp.einsum(
        "hts,thd->shd", grad_scores, query_heads, preferred_element_type=jnp.float32
    ) + last_f * jnp.einsum(
        "hde,she->shd", later_state, value_heads.astype(jnp.float32), precision=highest
    )
    value_grad = jnp.einsum(
        "hts,the->she", scores, grad_heads, preferred_element_type=jnp.float32
    ) + last_f * jnp.einsum(
        "hde,shd->she", later_state, key_heads.astype(jnp.float32), precision=highest
    )
    width = head_count * DH
    return (
        attended.reshape(tokens, width).astype(jnp.bfloat16),
        query_grad.reshape(tokens, width).astype(jnp.bfloat16),
        key_grad.reshape(tokens, width).astype(jnp.bfloat16),
        value_grad.reshape(tokens, width).astype(jnp.bfloat16),
    )


CHUNK_HEADS = 2


def bounded_kernel(
    count, lengths_ref, q_ref, k_ref, v_ref, g_ref,
    attended_ref, query_grad_ref, key_grad_ref, value_grad_ref,
    state, near, far, part, pair_mask, first_mask, last_mask,
    own_send, pass_send, far_send, near_recv, far_recv,
):
    tokens, width = q_ref.shape
    heads = width // DH
    chunks = heads // CHUNK_HEADS
    factor = (DH * tokens * count / DOCS) ** -0.5
    block = lax.axis_index("seq")
    parity = lax.rem(block, 2)
    partner = block + 1 - 2 * parity
    behind = block >= 2
    ahead = block + 2 < count
    takes = jnp.where(parity == 0, behind, ahead)
    passes = jnp.where(parity == 0, ahead, behind)

    barrier = pltpu.get_barrier_semaphore()
    pl.semaphore_signal(barrier, inc=1, device_id={"seq": partner})

    @pl.when(behind)
    def _():
        pl.semaphore_signal(barrier, inc=1, device_id={"seq": block - 2})

    @pl.when(ahead)
    def _():
        pl.semaphore_signal(barrier, inc=1, device_id={"seq": block + 2})

    first_pos = block * tokens
    rows = lax.broadcasted_iota(jnp.int32, (tokens, tokens), 0)
    columns = lax.broadcasted_iota(jnp.int32, (tokens, tokens), 1)
    row_doc = jnp.zeros((tokens, tokens), jnp.int32)
    column_doc = jnp.zeros((tokens, tokens), jnp.int32)
    zero, one = jnp.int32(0), jnp.int32(1)
    first_doc = last_doc = opens_first = opens_next = zero
    opens_before = opens_after = zero
    end = zero
    for doc in range(DOCS):
        start = end - first_pos
        end = end + lengths_ref[doc]
        stop = end - first_pos
        row_doc += jnp.where(stop <= rows, 1, 0)
        column_doc += jnp.where(stop <= columns, 1, 0)
        first_doc += jnp.where(stop <= 0, one, zero)
        last_doc += jnp.where(stop <= tokens - 1, one, zero)
        opens_first = jnp.maximum(opens_first, jnp.where(start == 0, one, zero))
        opens_next = jnp.maximum(opens_next, jnp.where(start == tokens, one, zero))
        before = (start >= -tokens) & (start < 0)
        after = (start >= tokens) & (start < 2 * tokens)
        opens_before = jnp.maximum(opens_before, jnp.where(before, one, zero))
        opens_after = jnp.maximum(opens_after, jnp.where(after, one, zero))
    near_weight = [
        factor * (1 - opens_first).astype(jnp.float32),
        factor * (1 - opens_next).astype(jnp.float32),
    ]
    far_weight = [
        near_weight[0] * (1 - opens_before).astype(jnp.float32),
        near_weight[1] * (1 - opens_after).astype(jnp.float32),
    ]
    pair_mask[...] = jnp.where((columns <= rows) & (row_doc == column_doc), factor, 0.0)
    first_mask[...] = jnp.where(row_doc == first_doc, 1.0, 0.0).astype(jnp.bfloat16)
    last_mask[...] = jnp.where(row_doc == last_doc, 1.0, 0.0).astype(jnp.bfloat16)

    def span(i):
        return pl.ds(i * CHUNK_HEADS, CHUNK_HEADS)

    def lanes(h):
        return pl.ds(pl.multiple_of(h * DH, DH), DH)

    def dot(a, b, dims):
        return lax.dot_general(a, b, (dims, ((), ())), preferred_element_type=jnp.float32)

    rows_rows, plain, turned = ((0,), (0,)), ((1,), (0,)), ((1,), (1,))

    def own_copy(i):
        return pltpu.make_async_remote_copy(
            state.at[parity, span(i)], near.at[parity, span(i)],
            own_send.at[i], near_recv.at[parity, i], device_id={"seq": partner},
        )

    def pass_copy(i):
        return pltpu.make_async_remote_copy(
            far.at[1 - parity, span(i)], near.at[1 - parity, span(i)],
            pass_send.at[i], near_recv.at[1 - parity, i], device_id={"seq": partner},
        )

    def far_copy(kind, i):
        return pltpu.make_async_remote_copy(
            state.at[kind, span(i)], far.at[kind, span(i)],
            far_send.at[kind, i], far_recv.at[kind, i],
            device_id={"seq": block + 2 - 4 * kind},
        )

    def states(i):
        for j in range(CHUNK_HEADS):
            h = i * CHUNK_HEADS + j
            at = lanes(h)
            state[0, h] = dot(k_ref[:, at] * last_mask[...], v_ref[:, at], rows_rows)
            state[1, h] = dot(q_ref[:, at] * first_mask[...], g_ref[:, at], rows_rows)

    def send(i):
        @pl.when(ahead)
        def _():
            far_copy(0, i).start()

        @pl.when(behind)
        def _():
            far_copy(1, i).start()

        own_copy(i).start()

    states(0)
    pl.semaphore_wait(
        barrier, 1 + jnp.where(behind, one, zero) + jnp.where(ahead, one, zero)
    )
    send(0)

    @pl.loop(1, chunks)
    def _(i):
        states(i)
        send(i)

    @pl.when(jnp.logical_not(takes))
    def _():
        @pl.loop(0, heads)
        def _(h):
            near[parity, h] = jnp.zeros((DH, DH), jnp.float32)
            far[parity, h] = jnp.zeros((DH, DH), jnp.float32)

    @pl.when(jnp.logical_not(passes))
    def _():
        @pl.loop(0, heads)
        def _(h):
            far[1 - parity, h] = jnp.zeros((DH, DH), jnp.float32)

    @pl.loop(0, chunks)
    def _(i):
        for j in range(CHUNK_HEADS):
            h = i * CHUNK_HEADS + j
            at = lanes(h)
            q, k, v, g = q_ref[:, at], k_ref[:, at], v_ref[:, at], g_ref[:, at]
            scores = (dot(q, k, turned) * pair_mask[...]).astype(jnp.bfloat16)
            grads = (dot(g, v, turned) * pair_mask[...]).astype(jnp.bfloat16)
            part[0, h] = dot(scores, v, plain)
            part[1, h] = dot(grads, k, plain)
            part[2, h] = dot(grads, q, rows_rows)
            part[3, h] = dot(scores, g, rows_rows)

        @pl.when(passes)
        def _():
            far_copy(1 - parity, i).wait_recv()
            pass_copy(i).start()

    @pl.loop(0, chunks)
    def _(i):
        own_copy(i).wait_send()

        @pl.when(ahead)
        def _():
            far_copy(0, i).wait_send()

        @pl.when(behind)
        def _():
            far_copy(1, i).wait_send()

        pass_copy(i).wait_recv()

        @pl.when(takes)
        def _():
            far_copy(parity, i).wait_recv()
            own_copy(i).wait_recv()

        for j in range(CHUNK_HEADS):
            h = i * CHUNK_HEADS + j
            at = lanes(h)
            mixed = []
            for kind in range(2):
                whole = near_weight[kind] * near[kind, h] + far_weight[kind] * far[kind, h]
                high = whole.astype(jnp.bfloat16)
                low = (whole - high.astype(jnp.float32)).astype(jnp.bfloat16)
                mixed.append((high, low))
            (prior, prior_low), (later, later_low) = mixed
            q, g = q_ref[:, at] * first_mask[...], g_ref[:, at] * first_mask[...]
            k, v = k_ref[:, at] * last_mask[...], v_ref[:, at] * last_mask[...]
            attended_ref[:, at] = (
                part[0, h] + (dot(q, prior, plain) + dot(q, prior_low, plain))
            ).astype(jnp.bfloat16)
            query_grad_ref[:, at] = (
                part[1, h] + (dot(g, prior, turned) + dot(g, prior_low, turned))
            ).astype(jnp.bfloat16)
            key_grad_ref[:, at] = (
                part[2, h] + (dot(v, later, turned) + dot(v, later_low, turned))
            ).astype(jnp.bfloat16)
            value_grad_ref[:, at] = (
                part[3, h] + (dot(k, later, plain) + dot(k, later_low, plain))
            ).astype(jnp.bfloat16)

    @pl.when(passes)
    def _():
        @pl.loop(0, chunks)
        def _(i):
            pass_copy(i).wait_send()


def local_bounded(queries, key_rows, value_rows, out_grad, lengths):
    tokens, width = queries.shape
    heads = width // DH
    chunks = heads // CHUNK_HEADS
    whole = pl.BlockSpec(memory_space=pltpu.VMEM)
    states = pltpu.VMEM((2, heads, DH, DH), jnp.float32)
    return tuple(pl.pallas_call(
        functools.partial(bounded_kernel, lax.axis_size("seq")),
        out_shape=[jax.ShapeDtypeStruct((tokens, width), jnp.bfloat16)] * 4,
        in_specs=[pl.BlockSpec(memory_space=pltpu.SMEM)] + [whole] * 4,
        out_specs=[whole] * 4,
        scratch_shapes=[
            states, states, states,
            pltpu.VMEM((4, heads, tokens, DH), jnp.float32),
            pltpu.VMEM((tokens, tokens), jnp.float32),
            pltpu.VMEM((tokens, DH), jnp.bfloat16),
            pltpu.VMEM((tokens, DH), jnp.bfloat16),
            pltpu.SemaphoreType.DMA((chunks,)),
            pltpu.SemaphoreType.DMA((chunks,)),
            pltpu.SemaphoreType.DMA((2, chunks)),
            pltpu.SemaphoreType.DMA((2, chunks)),
            pltpu.SemaphoreType.DMA((2, chunks)),
        ],
        compiler_params=pltpu.CompilerParams(
            collective_id=0, has_side_effects=True, vmem_limit_bytes=40 * 2**20
        ),
    )(lengths, queries, key_rows, value_rows, out_grad))


def local(queries, key_rows, value_rows, out_grad, lengths):
    count = lax.axis_size("seq")
    if count == 8 and queries.shape[0] == DH:
        return local_bounded(queries, key_rows, value_rows, out_grad, lengths)
    return local_general(queries, key_rows, value_rows, out_grad, lengths)


def solution(mesh):
    placed = (
        P(("groups", "seq"), "head"),
        P(("groups", "seq"), "head"),
        P(("groups", "seq"), "head"),
        P(("groups", "seq"), "head"),
        P("groups"),
    )
    return jax.shard_map(
        local,
        mesh=mesh,
        in_specs=placed,
        out_specs=(
            P(("groups", "seq"), "head"),
            P(("groups", "seq"), "head"),
            P(("groups", "seq"), "head"),
            P(("groups", "seq"), "head"),
        ),
        check_vma=False,
    )
```

```python
import functools

import jax
import jax.numpy as jnp
from jax import lax
from jax.experimental import pallas as pl
from jax.experimental.pallas import tpu as pltpu
from jax.sharding import PartitionSpec as P

DH = 128
DOCS = 16


def from_behind(block, axis, distance):
    devices = range(lax.axis_size(axis))
    route = [(i - distance, i) for i in devices if i - distance in devices]
    return lax.ppermute(block, axis, route)


def combine_pair(earlier, latter):
    return (earlier[0] * latter[0], latter[1] + latter[0] * earlier[1])


def prior_bounded(keep_gate, state, levels):
    distances = [1] + [1 << level for level in range(levels)]
    current = (keep_gate, state)
    for counter, distance in enumerate(distances):
        shifted = from_behind((current[0], current[1]), "seq", distance)
        if counter == 0:
            current = shifted
        else:
            current = combine_pair(shifted, current)
    return current[1]


def later_bounded(keep_gate, state, levels):
    distances = [1] + [1 << level for level in range(levels)]
    current = (keep_gate, state)
    for counter, distance in enumerate(distances):
        shifted = from_behind((current[0], current[1]), "seq", -distance)
        if counter == 0:
            current = shifted
        else:
            current = combine_pair(shifted, current)
    return current[1]


def local_general(queries, key_rows, value_rows, out_grad, lengths):
    tokens = queries.shape[0]
    head_count = queries.shape[1] // DH
    shape3 = (tokens, head_count, DH)
    highest = lax.Precision.HIGHEST
    query_heads = queries.reshape(shape3)
    key_heads = key_rows.reshape(shape3)
    value_heads = value_rows.reshape(shape3)
    grad_heads = out_grad.reshape(shape3)
    block_index = lax.axis_index("seq")
    doc_total = jnp.sum(lengths).astype(jnp.float32)
    factor = lax.rsqrt(jnp.float32(DH) * doc_total / DOCS)
    upto = jnp.tri(lengths.shape[0], dtype=jnp.int32)
    doc_ends = jnp.sum(upto * lengths[None, :], axis=1)
    doc_starts = doc_ends - lengths
    first_pos = block_index * tokens
    positions = first_pos + jnp.arange(tokens, dtype=jnp.int32)
    doc_ids = jnp.sum((doc_ends[None, :] <= positions[:, None]).astype(jnp.int32), axis=1)
    opens = jnp.any(doc_starts[None, :] == positions[:, None], axis=1)
    keep_gate = 1.0 - jnp.any(opens).astype(jnp.float32)
    open_here = opens[0].astype(jnp.float32)
    open_next = jnp.any(doc_starts == first_pos + tokens).astype(jnp.float32)
    first_mask = doc_ids == doc_ids[0]
    last_mask = doc_ids == doc_ids[-1]
    local_mask = (positions[None, :] <= positions[:, None]) & (doc_ids[:, None] == doc_ids[None, :])
    zero_half = jnp.zeros((), jnp.bfloat16)
    forward_state = jnp.einsum(
        "shd,she->hde",
        jnp.where(last_mask[:, None, None], key_heads, zero_half),
        value_heads,
        preferred_element_type=jnp.float32,
    )
    backward_state = jnp.einsum(
        "thd,the->hde",
        jnp.where(first_mask[:, None, None], query_heads, zero_half),
        grad_heads,
        preferred_element_type=jnp.float32,
    )
    levels = max(lax.axis_size("seq") // 4 - 1, 0).bit_length()
    prior = prior_bounded(keep_gate, forward_state, levels)
    later_state = later_bounded(keep_gate, backward_state, levels)
    prior = prior * (1.0 - open_here)
    later_state = later_state * (1.0 - open_next)
    first_f = factor * first_mask.astype(jnp.float32)[:, None, None]
    last_f = factor * last_mask.astype(jnp.float32)[:, None, None]
    raw_scores = jnp.einsum(
        "thd,shd->hts", query_heads, key_heads, preferred_element_type=jnp.float32
    )
    scores = jnp.where(local_mask[None], factor * raw_scores, 0.0).astype(jnp.bfloat16)
    attended = jnp.einsum(
        "hts,she->the", scores, value_heads, preferred_element_type=jnp.float32
    ) + first_f * jnp.einsum(
        "thd,hde->the", query_heads.astype(jnp.float32), prior, precision=highest
    )
    raw_grad = jnp.einsum(
        "the,she->hts", grad_heads, value_heads, preferred_element_type=jnp.float32
    )
    grad_scores = jnp.where(local_mask[None], factor * raw_grad, 0.0).astype(jnp.bfloat16)
    query_grad = jnp.einsum(
        "hts,shd->thd", grad_scores, key_heads, preferred_element_type=jnp.float32
    ) + first_f * jnp.einsum(
        "the,hde->thd", grad_heads.astype(jnp.float32), prior, precision=highest
    )
    key_grad = jnp.einsum(
        "hts,thd->shd", grad_scores, query_heads, preferred_element_type=jnp.float32
    ) + last_f * jnp.einsum(
        "hde,she->shd", later_state, value_heads.astype(jnp.float32), precision=highest
    )
    value_grad = jnp.einsum(
        "hts,the->she", scores, grad_heads, preferred_element_type=jnp.float32
    ) + last_f * jnp.einsum(
        "hde,shd->she", later_state, key_heads.astype(jnp.float32), precision=highest
    )
    width = head_count * DH
    return (
        attended.reshape(tokens, width).astype(jnp.bfloat16),
        query_grad.reshape(tokens, width).astype(jnp.bfloat16),
        key_grad.reshape(tokens, width).astype(jnp.bfloat16),
        value_grad.reshape(tokens, width).astype(jnp.bfloat16),
    )


CHUNK_HEADS = 2


def bounded_kernel(
    count, lengths_hbm, q_hbm, k_hbm, v_hbm, g_hbm,
    attended_ref, query_grad_ref, key_grad_ref, value_grad_ref,
    lengths_ref, q_ref, k_ref, v_ref, g_ref,
    state, near, far, aside, part, pair_mask, first_mask, last_mask,
    load, own_send, pass_send, aside_send, relay_send, aside_recv,
    far_send, near_recv, far_recv,
):
    tokens, width = q_ref.shape
    heads = width // DH
    chunks = heads // CHUNK_HEADS
    factor = (DH * tokens * count / DOCS) ** -0.5
    block = lax.axis_index("seq")
    parity = lax.rem(block, 2)
    partner = block + 1 - 2 * parity
    behind = block >= 2
    ahead = block + 2 < count
    takes = jnp.where(parity == 0, behind, ahead)
    passes = jnp.where(parity == 0, ahead, behind)

    row, row_count = lax.div(block, 2), count // 2
    onward = block + 2 - 4 * parity
    aside_end = jnp.where(parity == 0, row, row_count - 1 - row) * chunks // row_count
    relay_end = jnp.where(parity == 0, row_count - 1 - row, row) * chunks // row_count
    pass_start = jnp.where(parity == 0, row + 1, row_count - row) * chunks // row_count

    loads = [
        pltpu.make_async_copy(source, target, load.at[n])
        for n, (source, target) in enumerate([
            (lengths_hbm, lengths_ref), (k_hbm, k_ref), (v_hbm, v_ref),
            (q_hbm, q_ref), (g_hbm, g_ref),
        ])
    ]
    for copy in loads:
        copy.start()

    barrier = pltpu.get_barrier_semaphore()
    pl.semaphore_signal(barrier, inc=1, device_id={"seq": partner})

    @pl.when(behind)
    def _():
        pl.semaphore_signal(barrier, inc=1, device_id={"seq": block - 2})

    @pl.when(ahead)
    def _():
        pl.semaphore_signal(barrier, inc=1, device_id={"seq": block + 2})

    loads[0].wait()
    first_pos = block * tokens
    rows = lax.broadcasted_iota(jnp.int32, (tokens, tokens), 0)
    columns = lax.broadcasted_iota(jnp.int32, (tokens, tokens), 1)
    row_doc = jnp.zeros((tokens, tokens), jnp.int32)
    column_doc = jnp.zeros((tokens, tokens), jnp.int32)
    zero, one = jnp.int32(0), jnp.int32(1)
    first_doc = last_doc = opens_first = opens_next = zero
    opens_before = opens_after = zero
    end = zero
    for doc in range(DOCS):
        start = end - first_pos
        end = end + lengths_ref[doc]
        stop = end - first_pos
        row_doc += jnp.where(stop <= rows, 1, 0)
        column_doc += jnp.where(stop <= columns, 1, 0)
        first_doc += jnp.where(stop <= 0, one, zero)
        last_doc += jnp.where(stop <= tokens - 1, one, zero)
        opens_first = jnp.maximum(opens_first, jnp.where(start == 0, one, zero))
        opens_next = jnp.maximum(opens_next, jnp.where(start == tokens, one, zero))
        before = (start >= -tokens) & (start < 0)
        after = (start >= tokens) & (start < 2 * tokens)
        opens_before = jnp.maximum(opens_before, jnp.where(before, one, zero))
        opens_after = jnp.maximum(opens_after, jnp.where(after, one, zero))
    near_weight = [
        factor * (1 - opens_first).astype(jnp.float32),
        factor * (1 - opens_next).astype(jnp.float32),
    ]
    far_weight = [
        near_weight[0] * (1 - opens_before).astype(jnp.float32),
        near_weight[1] * (1 - opens_after).astype(jnp.float32),
    ]
    pair_mask[...] = jnp.where((columns <= rows) & (row_doc == column_doc), factor, 0.0)
    first_mask[...] = jnp.where(row_doc == first_doc, 1.0, 0.0).astype(jnp.bfloat16)
    last_mask[...] = jnp.where(row_doc == last_doc, 1.0, 0.0).astype(jnp.bfloat16)

    def span(i):
        return pl.ds(i * CHUNK_HEADS, CHUNK_HEADS)

    def lanes(h):
        return pl.ds(pl.multiple_of(h * DH, DH), DH)

    def dot(a, b, dims):
        return lax.dot_general(a, b, (dims, ((), ())), preferred_element_type=jnp.float32)

    rows_rows, plain, turned = ((0,), (0,)), ((1,), (0,)), ((1,), (1,))

    def own_copy(i):
        return pltpu.make_async_remote_copy(
            state.at[parity, span(i)], near.at[parity, span(i)],
            own_send.at[i], near_recv.at[parity, i], device_id={"seq": partner},
        )

    def pass_copy(i):
        return pltpu.make_async_remote_copy(
            far.at[1 - parity, span(i)], near.at[1 - parity, span(i)],
            pass_send.at[i], near_recv.at[1 - parity, i], device_id={"seq": partner},
        )

    def aside_copy(i):
        return pltpu.make_async_remote_copy(
            state.at[1 - parity, span(i)], aside.at[span(i)],
            aside_send.at[i], aside_recv.at[i], device_id={"seq": partner},
        )

    def relay_copy(i):
        return pltpu.make_async_remote_copy(
            aside.at[span(i)], near.at[parity, span(i)],
            relay_send.at[i], near_recv.at[parity, i], device_id={"seq": onward},
        )

    def far_copy(kind, i):
        return pltpu.make_async_remote_copy(
            state.at[kind, span(i)], far.at[kind, span(i)],
            far_send.at[kind, i], far_recv.at[kind, i],
            device_id={"seq": block + 2 - 4 * kind},
        )

    def states(i):
        for j in range(CHUNK_HEADS):
            h = i * CHUNK_HEADS + j
            at = lanes(h)
            state[0, h] = dot(k_ref[:, at] * last_mask[...], v_ref[:, at], rows_rows)
            state[1, h] = dot(q_ref[:, at] * first_mask[...], g_ref[:, at], rows_rows)

    def send(i):
        @pl.when(ahead)
        def _():
            far_copy(0, i).start()

        @pl.when(behind)
        def _():
            far_copy(1, i).start()

        @pl.when(i < aside_end)
        def _():
            aside_copy(i).start()

        own_copy(i).start()

    for copy in loads[1:]:
        copy.wait()
    states(0)
    neighbours = jnp.where(behind, one, zero) + jnp.where(ahead, one, zero)
    pl.semaphore_wait(barrier, 1 + neighbours)
    send(0)

    @pl.loop(1, chunks)
    def _(i):
        states(i)
        send(i)

    @pl.when(jnp.logical_not(takes))
    def _():
        @pl.loop(0, heads)
        def _(h):
            near[parity, h] = jnp.zeros((DH, DH), jnp.float32)
            far[parity, h] = jnp.zeros((DH, DH), jnp.float32)

    @pl.when(jnp.logical_not(passes))
    def _():
        @pl.loop(0, heads)
        def _(h):
            far[1 - parity, h] = jnp.zeros((DH, DH), jnp.float32)

    @pl.loop(0, chunks)
    def _(i):
        for j in range(CHUNK_HEADS):
            h = i * CHUNK_HEADS + j
            at = lanes(h)
            q, k, v, g = q_ref[:, at], k_ref[:, at], v_ref[:, at], g_ref[:, at]
            scores = (dot(q, k, turned) * pair_mask[...]).astype(jnp.bfloat16)
            grads = (dot(g, v, turned) * pair_mask[...]).astype(jnp.bfloat16)
            part[0, h] = dot(scores, v, plain)
            part[1, h] = dot(grads, k, plain)
            part[2, h] = dot(grads, q, rows_rows)
            part[3, h] = dot(scores, g, rows_rows)

        @pl.when(i < relay_end)
        def _():
            aside_copy(i).wait_recv()
            relay_copy(i).start()

        @pl.when(i + pass_start < chunks)
        def _():
            far_copy(1 - parity, i + pass_start).wait_recv()
            pass_copy(i + pass_start).start()

    @pl.loop(0, chunks)
    def _(i):
        pass_copy(i).wait_recv()

        @pl.when(passes & (i < pass_start))
        def _():
            far_copy(1 - parity, i).wait_recv()

        @pl.when(takes)
        def _():
            far_copy(parity, i).wait_recv()
            own_copy(i).wait_recv()

        for j in range(CHUNK_HEADS):
            h = i * CHUNK_HEADS + j
            at = lanes(h)
            mixed = []
            for kind in range(2):
                whole = near_weight[kind] * near[kind, h] + far_weight[kind] * far[kind, h]
                high = whole.astype(jnp.bfloat16)
                low = (whole - high.astype(jnp.float32)).astype(jnp.bfloat16)
                mixed.append((high, low))
            (prior, prior_low), (later, later_low) = mixed
            q, g = q_ref[:, at] * first_mask[...], g_ref[:, at] * first_mask[...]
            k, v = k_ref[:, at] * last_mask[...], v_ref[:, at] * last_mask[...]
            attended_ref[:, at] = (
                part[0, h] + (dot(q, prior, plain) + dot(q, prior_low, plain))
            ).astype(jnp.bfloat16)
            query_grad_ref[:, at] = (
                part[1, h] + (dot(g, prior, turned) + dot(g, prior_low, turned))
            ).astype(jnp.bfloat16)
            key_grad_ref[:, at] = (
                part[2, h] + (dot(v, later, turned) + dot(v, later_low, turned))
            ).astype(jnp.bfloat16)
            value_grad_ref[:, at] = (
                part[3, h] + (dot(k, later, plain) + dot(k, later_low, plain))
            ).astype(jnp.bfloat16)

    @pl.loop(0, chunks)
    def _(i):
        own_copy(i).wait_send()

        @pl.when(ahead)
        def _():
            far_copy(0, i).wait_send()

        @pl.when(behind)
        def _():
            far_copy(1, i).wait_send()

        @pl.when(i < aside_end)
        def _():
            aside_copy(i).wait_send()

        @pl.when(i < relay_end)
        def _():
            relay_copy(i).wait_send()

        @pl.when(i >= pass_start)
        def _():
            pass_copy(i).wait_send()


def store_kernel(*refs):
    sources, targets, done = refs[:4], refs[4:8], refs[8]
    copies = [
        pltpu.make_async_copy(sources[n], targets[n], done.at[n]) for n in range(4)
    ]
    for copy in copies:
        copy.start()
    for copy in copies:
        copy.wait()


def local_bounded(queries, key_rows, value_rows, out_grad, lengths):
    tokens, width = queries.shape
    heads = width // DH
    chunks = heads // CHUNK_HEADS
    whole = pl.BlockSpec(memory_space=pltpu.VMEM)
    states = pltpu.VMEM((2, heads, DH, DH), jnp.float32)
    apart = pl.BlockSpec(memory_space=pltpu.HBM)
    rows = pltpu.VMEM((tokens, width), jnp.bfloat16)
    outs = [jax.ShapeDtypeStruct((tokens, width), jnp.bfloat16)] * 4
    results = pl.pallas_call(
        functools.partial(bounded_kernel, lax.axis_size("seq")),
        out_shape=[pltpu.VMEM((tokens, width), jnp.bfloat16)] * 4,
        in_specs=[apart] * 5,
        out_specs=[whole] * 4,
        scratch_shapes=[
            pltpu.SMEM((DOCS,), jnp.int32),
            rows, rows, rows, rows,
            states, states, states,
            pltpu.VMEM((heads, DH, DH), jnp.float32),
            pltpu.VMEM((4, heads, tokens, DH), jnp.float32),
            pltpu.VMEM((tokens, tokens), jnp.float32),
            pltpu.VMEM((tokens, DH), jnp.bfloat16),
            pltpu.VMEM((tokens, DH), jnp.bfloat16),
            pltpu.SemaphoreType.DMA((5,)),
            pltpu.SemaphoreType.DMA((chunks,)),
            pltpu.SemaphoreType.DMA((chunks,)),
            pltpu.SemaphoreType.DMA((chunks,)),
            pltpu.SemaphoreType.DMA((chunks,)),
            pltpu.SemaphoreType.DMA((chunks,)),
            pltpu.SemaphoreType.DMA((2, chunks)),
            pltpu.SemaphoreType.DMA((2, chunks)),
            pltpu.SemaphoreType.DMA((2, chunks)),
        ],
        compiler_params=pltpu.CompilerParams(
            collective_id=0, has_side_effects=True, vmem_limit_bytes=60 * 2**20
        ),
    )(lengths, queries, key_rows, value_rows, out_grad)
    return tuple(pl.pallas_call(
        store_kernel,
        out_shape=outs,
        in_specs=[pl.BlockSpec(memory_space=pl.ANY)] * 4,
        out_specs=[apart] * 4,
        scratch_shapes=[pltpu.SemaphoreType.DMA((4,))],
        compiler_params=pltpu.CompilerParams(vmem_limit_bytes=2**20),
        cost_estimate=pl.CostEstimate(
            flops=0, bytes_accessed=16 * tokens * width, transcendentals=0
        ),
    )(*results))


def local(queries, key_rows, value_rows, out_grad, lengths):
    count = lax.axis_size("seq")
    if count == 8 and queries.shape[0] == DH:
        return local_bounded(queries, key_rows, value_rows, out_grad, lengths)
    return local_general(queries, key_rows, value_rows, out_grad, lengths)


def solution(mesh):
    placed = (
        P(("groups", "seq"), "head"),
        P(("groups", "seq"), "head"),
        P(("groups", "seq"), "head"),
        P(("groups", "seq"), "head"),
        P("groups"),
    )
    return jax.shard_map(
        local,
        mesh=mesh,
        in_specs=placed,
        out_specs=(
            P(("groups", "seq"), "head"),
            P(("groups", "seq"), "head"),
            P(("groups", "seq"), "head"),
            P(("groups", "seq"), "head"),
        ),
        check_vma=False,
    )
```

```python
import functools

import jax
import jax.numpy as jnp
from jax import lax
from jax.experimental import pallas as pl
from jax.experimental.pallas import tpu as pltpu
from jax.sharding import PartitionSpec as P

DH = 128
DOCS = 16


def from_behind(block, axis, distance):
    devices = range(lax.axis_size(axis))
    route = [(i - distance, i) for i in devices if i - distance in devices]
    return lax.ppermute(block, axis, route)


def combine_pair(earlier, latter):
    return (earlier[0] * latter[0], latter[1] + latter[0] * earlier[1])


def prior_bounded(keep_gate, state, levels):
    distances = [1] + [1 << level for level in range(levels)]
    current = (keep_gate, state)
    for counter, distance in enumerate(distances):
        shifted = from_behind((current[0], current[1]), "seq", distance)
        if counter == 0:
            current = shifted
        else:
            current = combine_pair(shifted, current)
    return current[1]


def later_bounded(keep_gate, state, levels):
    distances = [1] + [1 << level for level in range(levels)]
    current = (keep_gate, state)
    for counter, distance in enumerate(distances):
        shifted = from_behind((current[0], current[1]), "seq", -distance)
        if counter == 0:
            current = shifted
        else:
            current = combine_pair(shifted, current)
    return current[1]


def local_general(queries, key_rows, value_rows, out_grad, lengths):
    tokens = queries.shape[0]
    head_count = queries.shape[1] // DH
    shape3 = (tokens, head_count, DH)
    highest = lax.Precision.HIGHEST
    query_heads = queries.reshape(shape3)
    key_heads = key_rows.reshape(shape3)
    value_heads = value_rows.reshape(shape3)
    grad_heads = out_grad.reshape(shape3)
    block_index = lax.axis_index("seq")
    doc_total = jnp.sum(lengths).astype(jnp.float32)
    factor = lax.rsqrt(jnp.float32(DH) * doc_total / DOCS)
    upto = jnp.tri(lengths.shape[0], dtype=jnp.int32)
    doc_ends = jnp.sum(upto * lengths[None, :], axis=1)
    doc_starts = doc_ends - lengths
    first_pos = block_index * tokens
    positions = first_pos + jnp.arange(tokens, dtype=jnp.int32)
    doc_ids = jnp.sum((doc_ends[None, :] <= positions[:, None]).astype(jnp.int32), axis=1)
    opens = jnp.any(doc_starts[None, :] == positions[:, None], axis=1)
    keep_gate = 1.0 - jnp.any(opens).astype(jnp.float32)
    open_here = opens[0].astype(jnp.float32)
    open_next = jnp.any(doc_starts == first_pos + tokens).astype(jnp.float32)
    first_mask = doc_ids == doc_ids[0]
    last_mask = doc_ids == doc_ids[-1]
    local_mask = (positions[None, :] <= positions[:, None]) & (doc_ids[:, None] == doc_ids[None, :])
    zero_half = jnp.zeros((), jnp.bfloat16)
    forward_state = jnp.einsum(
        "shd,she->hde",
        jnp.where(last_mask[:, None, None], key_heads, zero_half),
        value_heads,
        preferred_element_type=jnp.float32,
    )
    backward_state = jnp.einsum(
        "thd,the->hde",
        jnp.where(first_mask[:, None, None], query_heads, zero_half),
        grad_heads,
        preferred_element_type=jnp.float32,
    )
    levels = max(lax.axis_size("seq") // 4 - 1, 0).bit_length()
    prior = prior_bounded(keep_gate, forward_state, levels)
    later_state = later_bounded(keep_gate, backward_state, levels)
    prior = prior * (1.0 - open_here)
    later_state = later_state * (1.0 - open_next)
    first_f = factor * first_mask.astype(jnp.float32)[:, None, None]
    last_f = factor * last_mask.astype(jnp.float32)[:, None, None]
    raw_scores = jnp.einsum(
        "thd,shd->hts", query_heads, key_heads, preferred_element_type=jnp.float32
    )
    scores = jnp.where(local_mask[None], factor * raw_scores, 0.0).astype(jnp.bfloat16)
    attended = jnp.einsum(
        "hts,she->the", scores, value_heads, preferred_element_type=jnp.float32
    ) + first_f * jnp.einsum(
        "thd,hde->the", query_heads.astype(jnp.float32), prior, precision=highest
    )
    raw_grad = jnp.einsum(
        "the,she->hts", grad_heads, value_heads, preferred_element_type=jnp.float32
    )
    grad_scores = jnp.where(local_mask[None], factor * raw_grad, 0.0).astype(jnp.bfloat16)
    query_grad = jnp.einsum(
        "hts,shd->thd", grad_scores, key_heads, preferred_element_type=jnp.float32
    ) + first_f * jnp.einsum(
        "the,hde->thd", grad_heads.astype(jnp.float32), prior, precision=highest
    )
    key_grad = jnp.einsum(
        "hts,thd->shd", grad_scores, query_heads, preferred_element_type=jnp.float32
    ) + last_f * jnp.einsum(
        "hde,she->shd", later_state, value_heads.astype(jnp.float32), precision=highest
    )
    value_grad = jnp.einsum(
        "hts,the->she", scores, grad_heads, preferred_element_type=jnp.float32
    ) + last_f * jnp.einsum(
        "hde,shd->she", later_state, key_heads.astype(jnp.float32), precision=highest
    )
    width = head_count * DH
    return (
        attended.reshape(tokens, width).astype(jnp.bfloat16),
        query_grad.reshape(tokens, width).astype(jnp.bfloat16),
        key_grad.reshape(tokens, width).astype(jnp.bfloat16),
        value_grad.reshape(tokens, width).astype(jnp.bfloat16),
    )


CHUNK_HEADS = 4


def bounded_kernel(
    count, lengths_hbm, q_hbm, k_hbm, v_hbm, g_hbm,
    attended_ref, query_grad_ref, key_grad_ref, value_grad_ref,
    lengths_ref, q_ref, k_ref, v_ref, g_ref,
    state, near, far, aside, part, pair_mask, first_mask, last_mask,
    load, own_send, cross_send, aside_send, relay_send, aside_recv,
    far_send, near_recv, far_recv,
):
    tokens, width = q_ref.shape
    heads = width // DH
    chunks = heads // CHUNK_HEADS
    factor = (DH * tokens * count / DOCS) ** -0.5
    block = lax.axis_index("seq")
    parity = lax.rem(block, 2)
    partner = block + 1 - 2 * parity
    behind = block >= 2
    ahead = block + 2 < count
    takes = jnp.where(parity == 0, behind, ahead)
    passes = jnp.where(parity == 0, ahead, behind)

    row, row_count = lax.div(block, 2), count // 2
    onward = block + 2 - 4 * parity
    across = block - 1 + 2 * parity
    aside_end = jnp.where(parity == 0, row, row_count - 1 - row) * chunks // row_count
    relay_end = jnp.where(parity == 0, row_count - 1 - row, row) * chunks // row_count

    barrier = pltpu.get_barrier_semaphore()
    pl.semaphore_signal(barrier, inc=1, device_id={"seq": partner})

    @pl.when(behind)
    def _():
        pl.semaphore_signal(barrier, inc=1, device_id={"seq": block - 2})

    @pl.when(ahead)
    def _():
        pl.semaphore_signal(barrier, inc=1, device_id={"seq": block + 2})

    @pl.when(takes)
    def _():
        pl.semaphore_signal(barrier, inc=1, device_id={"seq": across})

    early = pl.ds(0, CHUNK_HEADS * DH)
    late = pl.ds(CHUNK_HEADS * DH, width - CHUNK_HEADS * DH)
    pairs = [(k_hbm, k_ref), (v_hbm, v_ref), (q_hbm, q_ref), (g_hbm, g_ref)]
    loads = [pltpu.make_async_copy(lengths_hbm, lengths_ref, load.at[0])] + [
        pltpu.make_async_copy(source.at[:, at], target.at[:, at], load.at[1 + n + m])
        for n, at in ((0, early), (4, late))
        for m, (source, target) in enumerate(pairs)
    ]
    for copy in loads:
        copy.start()

    loads[0].wait()
    first_pos = block * tokens
    rows = lax.broadcasted_iota(jnp.int32, (tokens, tokens), 0)
    zero, one = jnp.int32(0), jnp.int32(1)
    opens_first = opens_next = opens_before = opens_after = zero
    first_stop, last_start = jnp.int32(tokens), zero
    stops = []
    stop = -first_pos
    for doc in range(DOCS):
        start = stop
        stop = start + lengths_ref[doc]
        stops.append(stop)
        first_stop = jnp.where(stop > 0, jnp.minimum(first_stop, stop), first_stop)
        last_start = jnp.where(start < tokens, jnp.maximum(last_start, start), last_start)
        opens_first = jnp.where(start == 0, one, opens_first)
        opens_next = jnp.where(start == tokens, one, opens_next)
        opens_before = jnp.where((start >= -tokens) & (start < 0), one, opens_before)
        opens_after = jnp.where(
            (start >= tokens) & (start < 2 * tokens), one, opens_after
        )
    near_weight = [
        factor * (1 - opens_first).astype(jnp.float32),
        factor * (1 - opens_next).astype(jnp.float32),
    ]
    far_weight = [
        near_weight[0] * (1 - opens_before).astype(jnp.float32),
        near_weight[1] * (1 - opens_after).astype(jnp.float32),
    ]
    first_mask[...] = jnp.where(rows < first_stop, 1.0, 0.0).astype(jnp.bfloat16)
    last_mask[...] = jnp.where(rows >= last_start, 1.0, 0.0).astype(jnp.bfloat16)

    def span(i):
        return pl.ds(i * CHUNK_HEADS, CHUNK_HEADS)

    def lanes(h):
        return pl.ds(pl.multiple_of(h * DH, DH), DH)

    def dot(a, b, dims):
        return lax.dot_general(a, b, (dims, ((), ())), preferred_element_type=jnp.float32)

    rows_rows, plain, turned = ((0,), (0,)), ((1,), (0,)), ((1,), (1,))

    def own_copy(i):
        return pltpu.make_async_remote_copy(
            state.at[parity, span(i)], near.at[parity, span(i)],
            own_send.at[i], near_recv.at[parity, i], device_id={"seq": partner},
        )

    def cross_copy(i):
        return pltpu.make_async_remote_copy(
            state.at[1 - parity, span(i)], near.at[1 - parity, span(i)],
            cross_send.at[i], near_recv.at[1 - parity, i], device_id={"seq": across},
        )

    def aside_copy(i):
        return pltpu.make_async_remote_copy(
            state.at[1 - parity, span(i)], aside.at[span(i)],
            aside_send.at[i], aside_recv.at[i], device_id={"seq": partner},
        )

    def relay_copy(i):
        return pltpu.make_async_remote_copy(
            aside.at[span(i)], near.at[parity, span(i)],
            relay_send.at[i], near_recv.at[parity, i], device_id={"seq": onward},
        )

    def far_copy(kind, i):
        return pltpu.make_async_remote_copy(
            state.at[kind, span(i)], far.at[kind, span(i)],
            far_send.at[kind, i], far_recv.at[kind, i],
            device_id={"seq": block + 2 - 4 * kind},
        )

    def states(i):
        for j in range(CHUNK_HEADS):
            h = i * CHUNK_HEADS + j
            at = lanes(h)
            state[0, h] = dot(k_ref[:, at] * last_mask[...], v_ref[:, at], rows_rows)
            state[1, h] = dot(q_ref[:, at] * first_mask[...], g_ref[:, at], rows_rows)

    def send(i):
        @pl.when(ahead)
        def _():
            far_copy(0, i).start()

        @pl.when(behind)
        def _():
            far_copy(1, i).start()

        @pl.when(i < aside_end)
        def _():
            aside_copy(i).start()

        @pl.when(takes & (i >= aside_end))
        def _():
            cross_copy(i).start()

        own_copy(i).start()

    for copy in loads[1:5]:
        copy.wait()
    states(0)
    neighbours = jnp.where(behind, one, zero) + jnp.where(ahead, one, zero)
    pl.semaphore_wait(barrier, 1 + neighbours + jnp.where(takes, one, zero))
    send(0)
    for copy in loads[5:]:
        copy.wait()

    @pl.loop(1, chunks)
    def _(i):
        states(i)
        send(i)

    columns = lax.broadcasted_iota(jnp.int32, (tokens, tokens), 1)
    row_doc = jnp.zeros((tokens, tokens), jnp.int32)
    column_doc = jnp.zeros((tokens, tokens), jnp.int32)
    for stop in stops:
        row_doc += jnp.where(stop <= rows, 1, 0)
        column_doc += jnp.where(stop <= columns, 1, 0)
    pair_mask[...] = jnp.where((columns <= rows) & (row_doc == column_doc), factor, 0.0)

    @pl.when(jnp.logical_not(takes))
    def _():
        @pl.loop(0, heads)
        def _(h):
            near[parity, h] = jnp.zeros((DH, DH), jnp.float32)
            far[parity, h] = jnp.zeros((DH, DH), jnp.float32)

    @pl.when(jnp.logical_not(passes))
    def _():
        @pl.loop(0, heads)
        def _(h):
            far[1 - parity, h] = jnp.zeros((DH, DH), jnp.float32)

    @pl.loop(0, chunks)
    def _(i):
        for j in range(CHUNK_HEADS):
            h = i * CHUNK_HEADS + j
            at = lanes(h)
            q, k, v, g = q_ref[:, at], k_ref[:, at], v_ref[:, at], g_ref[:, at]
            scores = (dot(q, k, turned) * pair_mask[...]).astype(jnp.bfloat16)
            grads = (dot(g, v, turned) * pair_mask[...]).astype(jnp.bfloat16)
            part[0, h] = dot(scores, v, plain)
            part[1, h] = dot(grads, k, plain)
            part[2, h] = dot(grads, q, rows_rows)
            part[3, h] = dot(scores, g, rows_rows)

        @pl.when(i < relay_end)
        def _():
            aside_copy(i).wait_recv()
            relay_copy(i).start()

    @pl.loop(0, chunks)
    def _(i):
        cross_copy(i).wait_recv()

        @pl.when(passes)
        def _():
            far_copy(1 - parity, i).wait_recv()

        @pl.when(takes)
        def _():
            far_copy(parity, i).wait_recv()
            own_copy(i).wait_recv()

        for j in range(CHUNK_HEADS):
            h = i * CHUNK_HEADS + j
            at = lanes(h)
            mixed = []
            for kind in range(2):
                whole = near_weight[kind] * near[kind, h] + far_weight[kind] * far[kind, h]
                high = whole.astype(jnp.bfloat16)
                low = (whole - high.astype(jnp.float32)).astype(jnp.bfloat16)
                mixed.append((high, low))
            (prior, prior_low), (later, later_low) = mixed
            q, g = q_ref[:, at] * first_mask[...], g_ref[:, at] * first_mask[...]
            k, v = k_ref[:, at] * last_mask[...], v_ref[:, at] * last_mask[...]
            attended_ref[:, at] = (
                part[0, h] + (dot(q, prior, plain) + dot(q, prior_low, plain))
            ).astype(jnp.bfloat16)
            query_grad_ref[:, at] = (
                part[1, h] + (dot(g, prior, turned) + dot(g, prior_low, turned))
            ).astype(jnp.bfloat16)
            key_grad_ref[:, at] = (
                part[2, h] + (dot(v, later, turned) + dot(v, later_low, turned))
            ).astype(jnp.bfloat16)
            value_grad_ref[:, at] = (
                part[3, h] + (dot(k, later, plain) + dot(k, later_low, plain))
            ).astype(jnp.bfloat16)

    @pl.loop(0, chunks)
    def _(i):
        own_copy(i).wait_send()

        @pl.when(ahead)
        def _():
            far_copy(0, i).wait_send()

        @pl.when(behind)
        def _():
            far_copy(1, i).wait_send()

        @pl.when(i < aside_end)
        def _():
            aside_copy(i).wait_send()

        @pl.when(i < relay_end)
        def _():
            relay_copy(i).wait_send()

        @pl.when(takes & (i >= aside_end))
        def _():
            cross_copy(i).wait_send()


def store_kernel(*refs):
    sources, targets, done = refs[:4], refs[4:8], refs[8]
    copies = [
        pltpu.make_async_copy(sources[n], targets[n], done.at[n]) for n in range(4)
    ]
    for copy in copies:
        copy.start()
    for copy in copies:
        copy.wait()


def local_bounded(queries, key_rows, value_rows, out_grad, lengths):
    tokens, width = queries.shape
    heads = width // DH
    chunks = heads // CHUNK_HEADS
    whole = pl.BlockSpec(memory_space=pltpu.VMEM)
    states = pltpu.VMEM((2, heads, DH, DH), jnp.float32)
    apart = pl.BlockSpec(memory_space=pltpu.HBM)
    rows = pltpu.VMEM((tokens, width), jnp.bfloat16)
    outs = [jax.ShapeDtypeStruct((tokens, width), jnp.bfloat16)] * 4
    results = pl.pallas_call(
        functools.partial(bounded_kernel, lax.axis_size("seq")),
        out_shape=[pltpu.VMEM((tokens, width), jnp.bfloat16)] * 4,
        in_specs=[apart] * 5,
        out_specs=[whole] * 4,
        scratch_shapes=[
            pltpu.SMEM((DOCS,), jnp.int32),
            rows, rows, rows, rows,
            states, states, states,
            pltpu.VMEM((heads, DH, DH), jnp.float32),
            pltpu.VMEM((4, heads, tokens, DH), jnp.float32),
            pltpu.VMEM((tokens, tokens), jnp.float32),
            pltpu.VMEM((tokens, DH), jnp.bfloat16),
            pltpu.VMEM((tokens, DH), jnp.bfloat16),
            pltpu.SemaphoreType.DMA((9,)),
            pltpu.SemaphoreType.DMA((chunks,)),
            pltpu.SemaphoreType.DMA((chunks,)),
            pltpu.SemaphoreType.DMA((chunks,)),
            pltpu.SemaphoreType.DMA((chunks,)),
            pltpu.SemaphoreType.DMA((chunks,)),
            pltpu.SemaphoreType.DMA((2, chunks)),
            pltpu.SemaphoreType.DMA((2, chunks)),
            pltpu.SemaphoreType.DMA((2, chunks)),
        ],
        compiler_params=pltpu.CompilerParams(
            collective_id=0, has_side_effects=True, vmem_limit_bytes=60 * 2**20
        ),
    )(lengths, queries, key_rows, value_rows, out_grad)
    return tuple(pl.pallas_call(
        store_kernel,
        out_shape=outs,
        in_specs=[pl.BlockSpec(memory_space=pl.ANY)] * 4,
        out_specs=[apart] * 4,
        scratch_shapes=[pltpu.SemaphoreType.DMA((4,))],
        compiler_params=pltpu.CompilerParams(vmem_limit_bytes=2**20),
        cost_estimate=pl.CostEstimate(
            flops=0, bytes_accessed=16 * tokens * width, transcendentals=0
        ),
    )(*results))


def local(queries, key_rows, value_rows, out_grad, lengths):
    count = lax.axis_size("seq")
    if count == 8 and queries.shape[0] == DH:
        return local_bounded(queries, key_rows, value_rows, out_grad, lengths)
    return local_general(queries, key_rows, value_rows, out_grad, lengths)


def solution(mesh):
    placed = (
        P(("groups", "seq"), "head"),
        P(("groups", "seq"), "head"),
        P(("groups", "seq"), "head"),
        P(("groups", "seq"), "head"),
        P("groups"),
    )
    return jax.shard_map(
        local,
        mesh=mesh,
        in_specs=placed,
        out_specs=(
            P(("groups", "seq"), "head"),
            P(("groups", "seq"), "head"),
            P(("groups", "seq"), "head"),
            P(("groups", "seq"), "head"),
        ),
        check_vma=False,
    )
```

```python
import functools

import jax
import jax.numpy as jnp
from jax import lax
from jax.experimental import pallas as pl
from jax.experimental.pallas import tpu as pltpu
from jax.sharding import PartitionSpec as P

DH = 128
DOCS = 16


def from_behind(block, axis, distance):
    devices = range(lax.axis_size(axis))
    route = [(i - distance, i) for i in devices if i - distance in devices]
    return lax.ppermute(block, axis, route)


def combine_pair(earlier, latter):
    return (earlier[0] * latter[0], latter[1] + latter[0] * earlier[1])


def prior_bounded(keep_gate, state, levels):
    distances = [1] + [1 << level for level in range(levels)]
    current = (keep_gate, state)
    for counter, distance in enumerate(distances):
        shifted = from_behind((current[0], current[1]), "seq", distance)
        if counter == 0:
            current = shifted
        else:
            current = combine_pair(shifted, current)
    return current[1]


def later_bounded(keep_gate, state, levels):
    distances = [1] + [1 << level for level in range(levels)]
    current = (keep_gate, state)
    for counter, distance in enumerate(distances):
        shifted = from_behind((current[0], current[1]), "seq", -distance)
        if counter == 0:
            current = shifted
        else:
            current = combine_pair(shifted, current)
    return current[1]


def local_general(queries, key_rows, value_rows, out_grad, lengths):
    tokens = queries.shape[0]
    head_count = queries.shape[1] // DH
    shape3 = (tokens, head_count, DH)
    highest = lax.Precision.HIGHEST
    query_heads = queries.reshape(shape3)
    key_heads = key_rows.reshape(shape3)
    value_heads = value_rows.reshape(shape3)
    grad_heads = out_grad.reshape(shape3)
    block_index = lax.axis_index("seq")
    doc_total = jnp.sum(lengths).astype(jnp.float32)
    factor = lax.rsqrt(jnp.float32(DH) * doc_total / DOCS)
    upto = jnp.tri(lengths.shape[0], dtype=jnp.int32)
    doc_ends = jnp.sum(upto * lengths[None, :], axis=1)
    doc_starts = doc_ends - lengths
    first_pos = block_index * tokens
    positions = first_pos + jnp.arange(tokens, dtype=jnp.int32)
    doc_ids = jnp.sum((doc_ends[None, :] <= positions[:, None]).astype(jnp.int32), axis=1)
    opens = jnp.any(doc_starts[None, :] == positions[:, None], axis=1)
    keep_gate = 1.0 - jnp.any(opens).astype(jnp.float32)
    open_here = opens[0].astype(jnp.float32)
    open_next = jnp.any(doc_starts == first_pos + tokens).astype(jnp.float32)
    first_mask = doc_ids == doc_ids[0]
    last_mask = doc_ids == doc_ids[-1]
    local_mask = (positions[None, :] <= positions[:, None]) & (doc_ids[:, None] == doc_ids[None, :])
    zero_half = jnp.zeros((), jnp.bfloat16)
    forward_state = jnp.einsum(
        "shd,she->hde",
        jnp.where(last_mask[:, None, None], key_heads, zero_half),
        value_heads,
        preferred_element_type=jnp.float32,
    )
    backward_state = jnp.einsum(
        "thd,the->hde",
        jnp.where(first_mask[:, None, None], query_heads, zero_half),
        grad_heads,
        preferred_element_type=jnp.float32,
    )
    levels = max(lax.axis_size("seq") // 4 - 1, 0).bit_length()
    prior = prior_bounded(keep_gate, forward_state, levels)
    later_state = later_bounded(keep_gate, backward_state, levels)
    prior = prior * (1.0 - open_here)
    later_state = later_state * (1.0 - open_next)
    first_f = factor * first_mask.astype(jnp.float32)[:, None, None]
    last_f = factor * last_mask.astype(jnp.float32)[:, None, None]
    raw_scores = jnp.einsum(
        "thd,shd->hts", query_heads, key_heads, preferred_element_type=jnp.float32
    )
    scores = jnp.where(local_mask[None], factor * raw_scores, 0.0).astype(jnp.bfloat16)
    attended = jnp.einsum(
        "hts,she->the", scores, value_heads, preferred_element_type=jnp.float32
    ) + first_f * jnp.einsum(
        "thd,hde->the", query_heads.astype(jnp.float32), prior, precision=highest
    )
    raw_grad = jnp.einsum(
        "the,she->hts", grad_heads, value_heads, preferred_element_type=jnp.float32
    )
    grad_scores = jnp.where(local_mask[None], factor * raw_grad, 0.0).astype(jnp.bfloat16)
    query_grad = jnp.einsum(
        "hts,shd->thd", grad_scores, key_heads, preferred_element_type=jnp.float32
    ) + first_f * jnp.einsum(
        "the,hde->thd", grad_heads.astype(jnp.float32), prior, precision=highest
    )
    key_grad = jnp.einsum(
        "hts,thd->shd", grad_scores, query_heads, preferred_element_type=jnp.float32
    ) + last_f * jnp.einsum(
        "hde,she->shd", later_state, value_heads.astype(jnp.float32), precision=highest
    )
    value_grad = jnp.einsum(
        "hts,the->she", scores, grad_heads, preferred_element_type=jnp.float32
    ) + last_f * jnp.einsum(
        "hde,shd->she", later_state, key_heads.astype(jnp.float32), precision=highest
    )
    width = head_count * DH
    return (
        attended.reshape(tokens, width).astype(jnp.bfloat16),
        query_grad.reshape(tokens, width).astype(jnp.bfloat16),
        key_grad.reshape(tokens, width).astype(jnp.bfloat16),
        value_grad.reshape(tokens, width).astype(jnp.bfloat16),
    )


SIZES = (1, 3, 4, 4, 2, 2)
STARTS = (0, 1, 4, 8, 12, 14)


def bounded_kernel(
    count, lengths_hbm, q_hbm, k_hbm, v_hbm, g_hbm,
    attended_ref, query_grad_ref, key_grad_ref, value_grad_ref,
    lengths_ref, q_ref, k_ref, v_ref, g_ref,
    state, near, far, aside, part, pair_mask, first_mask, last_mask,
    load, own_send, cross_send, aside_send, relay_send, aside_recv,
    far_send, near_recv, far_recv,
):
    tokens, width = q_ref.shape
    heads = width // DH
    chunks = len(SIZES)
    factor = (DH * tokens * count / DOCS) ** -0.5
    block = lax.axis_index("seq")
    parity = lax.rem(block, 2)
    partner = block + 1 - 2 * parity
    behind = block >= 2
    ahead = block + 2 < count
    takes = jnp.where(parity == 0, behind, ahead)
    passes = jnp.where(parity == 0, ahead, behind)

    row, row_count = lax.div(block, 2), count // 2
    onward = block + 2 - 4 * parity
    across = block - 1 + 2 * parity
    aside_end = jnp.where(parity == 0, row, row_count - 1 - row) * heads // row_count
    relay_end = jnp.where(parity == 0, row_count - 1 - row, row) * heads // row_count

    barrier = pltpu.get_barrier_semaphore()
    pl.semaphore_signal(barrier, inc=1, device_id={"seq": partner})

    @pl.when(behind)
    def _():
        pl.semaphore_signal(barrier, inc=1, device_id={"seq": block - 2})

    @pl.when(ahead)
    def _():
        pl.semaphore_signal(barrier, inc=1, device_id={"seq": block + 2})

    @pl.when(takes)
    def _():
        pl.semaphore_signal(barrier, inc=1, device_id={"seq": across})

    early = pl.ds(0, SIZES[0] * DH)
    late = pl.ds(SIZES[0] * DH, width - SIZES[0] * DH)
    pairs = [(k_hbm, k_ref), (v_hbm, v_ref), (q_hbm, q_ref), (g_hbm, g_ref)]
    loads = [pltpu.make_async_copy(lengths_hbm, lengths_ref, load.at[0])] + [
        pltpu.make_async_copy(source.at[:, at], target.at[:, at], load.at[1 + n + m])
        for n, at in ((0, early), (4, late))
        for m, (source, target) in enumerate(pairs)
    ]
    for copy in loads:
        copy.start()

    loads[0].wait()
    first_pos = block * tokens
    rows = lax.broadcasted_iota(jnp.int32, (tokens, tokens), 0)
    zero, one = jnp.int32(0), jnp.int32(1)
    opens_first = opens_next = opens_before = opens_after = zero
    first_stop, last_start = jnp.int32(tokens), zero
    stops = []
    stop = -first_pos
    for doc in range(DOCS):
        start = stop
        stop = start + lengths_ref[doc]
        stops.append(stop)
        first_stop = jnp.where(stop > 0, jnp.minimum(first_stop, stop), first_stop)
        last_start = jnp.where(start < tokens, jnp.maximum(last_start, start), last_start)
        opens_first = jnp.where(start == 0, one, opens_first)
        opens_next = jnp.where(start == tokens, one, opens_next)
        opens_before = jnp.where((start >= -tokens) & (start < 0), one, opens_before)
        opens_after = jnp.where(
            (start >= tokens) & (start < 2 * tokens), one, opens_after
        )
    near_weight = [
        factor * (1 - opens_first).astype(jnp.float32),
        factor * (1 - opens_next).astype(jnp.float32),
    ]
    far_weight = [
        near_weight[0] * (1 - opens_before).astype(jnp.float32),
        near_weight[1] * (1 - opens_after).astype(jnp.float32),
    ]
    first_mask[...] = jnp.where(rows < first_stop, 1.0, 0.0).astype(jnp.bfloat16)
    last_mask[...] = jnp.where(rows >= last_start, 1.0, 0.0).astype(jnp.bfloat16)

    def span(i):
        return pl.ds(STARTS[i], SIZES[i])

    def lanes(h):
        return pl.ds(h * DH, DH)

    def dot(a, b, dims):
        return lax.dot_general(a, b, (dims, ((), ())), preferred_element_type=jnp.float32)

    rows_rows, plain, turned = ((0,), (0,)), ((1,), (0,)), ((1,), (1,))

    def own_copy(i):
        return pltpu.make_async_remote_copy(
            state.at[parity, span(i)], near.at[parity, span(i)],
            own_send.at[i], near_recv.at[parity, i], device_id={"seq": partner},
        )

    def cross_copy(i):
        return pltpu.make_async_remote_copy(
            state.at[1 - parity, span(i)], near.at[1 - parity, span(i)],
            cross_send.at[i], near_recv.at[1 - parity, i], device_id={"seq": across},
        )

    def aside_copy(i):
        return pltpu.make_async_remote_copy(
            state.at[1 - parity, span(i)], aside.at[span(i)],
            aside_send.at[i], aside_recv.at[i], device_id={"seq": partner},
        )

    def relay_copy(i):
        return pltpu.make_async_remote_copy(
            aside.at[span(i)], near.at[parity, span(i)],
            relay_send.at[i], near_recv.at[parity, i], device_id={"seq": onward},
        )

    def far_copy(kind, i):
        return pltpu.make_async_remote_copy(
            state.at[kind, span(i)], far.at[kind, span(i)],
            far_send.at[kind, i], far_recv.at[kind, i],
            device_id={"seq": block + 2 - 4 * kind},
        )

    def states(i):
        for h in range(STARTS[i], STARTS[i] + SIZES[i]):
            at = lanes(h)
            state[0, h] = dot(k_ref[:, at] * last_mask[...], v_ref[:, at], rows_rows)
            state[1, h] = dot(q_ref[:, at] * first_mask[...], g_ref[:, at], rows_rows)

    def send(i):
        @pl.when(ahead)
        def _():
            far_copy(0, i).start()

        @pl.when(behind)
        def _():
            far_copy(1, i).start()

        @pl.when(STARTS[i] < aside_end)
        def _():
            aside_copy(i).start()

        @pl.when(takes & (STARTS[i] >= aside_end))
        def _():
            cross_copy(i).start()

        own_copy(i).start()

    for copy in loads[1:5]:
        copy.wait()
    states(0)
    neighbours = jnp.where(behind, one, zero) + jnp.where(ahead, one, zero)
    pl.semaphore_wait(barrier, 1 + neighbours + jnp.where(takes, one, zero))
    send(0)
    for copy in loads[5:]:
        copy.wait()

    for i in range(1, chunks):
        states(i)
        send(i)

    columns = lax.broadcasted_iota(jnp.int32, (tokens, tokens), 1)
    row_doc = jnp.zeros((tokens, tokens), jnp.int32)
    column_doc = jnp.zeros((tokens, tokens), jnp.int32)
    for stop in stops:
        row_doc += jnp.where(stop <= rows, 1, 0)
        column_doc += jnp.where(stop <= columns, 1, 0)
    pair_mask[...] = jnp.where((columns <= rows) & (row_doc == column_doc), factor, 0.0)

    @pl.when(jnp.logical_not(takes))
    def _():
        @pl.loop(0, heads)
        def _(h):
            near[parity, h] = jnp.zeros((DH, DH), jnp.float32)
            far[parity, h] = jnp.zeros((DH, DH), jnp.float32)

    @pl.when(jnp.logical_not(passes))
    def _():
        @pl.loop(0, heads)
        def _(h):
            far[1 - parity, h] = jnp.zeros((DH, DH), jnp.float32)

    for i in range(chunks):
        for h in range(STARTS[i], STARTS[i] + SIZES[i]):
            at = lanes(h)
            q, k, v, g = q_ref[:, at], k_ref[:, at], v_ref[:, at], g_ref[:, at]
            scores = (dot(q, k, turned) * pair_mask[...]).astype(jnp.bfloat16)
            grads = (dot(g, v, turned) * pair_mask[...]).astype(jnp.bfloat16)
            part[0, h] = dot(scores, v, plain)
            part[1, h] = dot(grads, k, plain)
            part[2, h] = dot(grads, q, rows_rows)
            part[3, h] = dot(scores, g, rows_rows)

        @pl.when(STARTS[i] < relay_end)
        def _():
            aside_copy(i).wait_recv()
            relay_copy(i).start()

    for i in range(chunks):
        cross_copy(i).wait_recv()

        @pl.when(passes)
        def _():
            far_copy(1 - parity, i).wait_recv()

        @pl.when(takes)
        def _():
            far_copy(parity, i).wait_recv()
            own_copy(i).wait_recv()

        for h in range(STARTS[i], STARTS[i] + SIZES[i]):
            at = lanes(h)
            mixed = []
            for kind in range(2):
                whole = near_weight[kind] * near[kind, h] + far_weight[kind] * far[kind, h]
                high = whole.astype(jnp.bfloat16)
                low = (whole - high.astype(jnp.float32)).astype(jnp.bfloat16)
                mixed.append((high, low))
            (prior, prior_low), (later, later_low) = mixed
            q, g = q_ref[:, at] * first_mask[...], g_ref[:, at] * first_mask[...]
            k, v = k_ref[:, at] * last_mask[...], v_ref[:, at] * last_mask[...]
            attended_ref[:, at] = (
                part[0, h] + (dot(q, prior, plain) + dot(q, prior_low, plain))
            ).astype(jnp.bfloat16)
            query_grad_ref[:, at] = (
                part[1, h] + (dot(g, prior, turned) + dot(g, prior_low, turned))
            ).astype(jnp.bfloat16)
            key_grad_ref[:, at] = (
                part[2, h] + (dot(v, later, turned) + dot(v, later_low, turned))
            ).astype(jnp.bfloat16)
            value_grad_ref[:, at] = (
                part[3, h] + (dot(k, later, plain) + dot(k, later_low, plain))
            ).astype(jnp.bfloat16)

    for i in range(chunks):
        own_copy(i).wait_send()

        @pl.when(ahead)
        def _():
            far_copy(0, i).wait_send()

        @pl.when(behind)
        def _():
            far_copy(1, i).wait_send()

        @pl.when(STARTS[i] < aside_end)
        def _():
            aside_copy(i).wait_send()

        @pl.when(STARTS[i] < relay_end)
        def _():
            relay_copy(i).wait_send()

        @pl.when(takes & (STARTS[i] >= aside_end))
        def _():
            cross_copy(i).wait_send()


def store_kernel(*refs):
    sources, targets, done = refs[:4], refs[4:8], refs[8]
    copies = [
        pltpu.make_async_copy(sources[n], targets[n], done.at[n]) for n in range(4)
    ]
    for copy in copies:
        copy.start()
    for copy in copies:
        copy.wait()


def local_bounded(queries, key_rows, value_rows, out_grad, lengths):
    tokens, width = queries.shape
    heads = width // DH
    chunks = len(SIZES)
    whole = pl.BlockSpec(memory_space=pltpu.VMEM)
    states = pltpu.VMEM((2, heads, DH, DH), jnp.float32)
    apart = pl.BlockSpec(memory_space=pltpu.HBM)
    rows = pltpu.VMEM((tokens, width), jnp.bfloat16)
    outs = [jax.ShapeDtypeStruct((tokens, width), jnp.bfloat16)] * 4
    results = pl.pallas_call(
        functools.partial(bounded_kernel, lax.axis_size("seq")),
        out_shape=[pltpu.VMEM((tokens, width), jnp.bfloat16)] * 4,
        in_specs=[apart] * 5,
        out_specs=[whole] * 4,
        scratch_shapes=[
            pltpu.SMEM((DOCS,), jnp.int32),
            rows, rows, rows, rows,
            states, states, states,
            pltpu.VMEM((heads, DH, DH), jnp.float32),
            pltpu.VMEM((4, heads, tokens, DH), jnp.float32),
            pltpu.VMEM((tokens, tokens), jnp.float32),
            pltpu.VMEM((tokens, DH), jnp.bfloat16),
            pltpu.VMEM((tokens, DH), jnp.bfloat16),
            pltpu.SemaphoreType.DMA((9,)),
            pltpu.SemaphoreType.DMA((chunks,)),
            pltpu.SemaphoreType.DMA((chunks,)),
            pltpu.SemaphoreType.DMA((chunks,)),
            pltpu.SemaphoreType.DMA((chunks,)),
            pltpu.SemaphoreType.DMA((chunks,)),
            pltpu.SemaphoreType.DMA((2, chunks)),
            pltpu.SemaphoreType.DMA((2, chunks)),
            pltpu.SemaphoreType.DMA((2, chunks)),
        ],
        compiler_params=pltpu.CompilerParams(
            collective_id=0, has_side_effects=True, vmem_limit_bytes=60 * 2**20
        ),
    )(lengths, queries, key_rows, value_rows, out_grad)
    return tuple(pl.pallas_call(
        store_kernel,
        out_shape=outs,
        in_specs=[pl.BlockSpec(memory_space=pl.ANY)] * 4,
        out_specs=[apart] * 4,
        scratch_shapes=[pltpu.SemaphoreType.DMA((4,))],
        compiler_params=pltpu.CompilerParams(vmem_limit_bytes=2**20),
        cost_estimate=pl.CostEstimate(
            flops=0, bytes_accessed=16 * tokens * width, transcendentals=0
        ),
    )(*results))


def local(queries, key_rows, value_rows, out_grad, lengths):
    count = lax.axis_size("seq")
    if count == 8 and queries.shape == (DH, 16 * DH):
        return local_bounded(queries, key_rows, value_rows, out_grad, lengths)
    return local_general(queries, key_rows, value_rows, out_grad, lengths)


def solution(mesh):
    placed = (
        P(("groups", "seq"), "head"),
        P(("groups", "seq"), "head"),
        P(("groups", "seq"), "head"),
        P(("groups", "seq"), "head"),
        P("groups"),
    )
    return jax.shard_map(
        local,
        mesh=mesh,
        in_specs=placed,
        out_specs=(
            P(("groups", "seq"), "head"),
            P(("groups", "seq"), "head"),
            P(("groups", "seq"), "head"),
            P(("groups", "seq"), "head"),
        ),
        check_vma=False,
    )
```
